128 devices in a mesh: expert: 8 (over y, core), dp: 16 (over x, z).
Axes of the slice: x: 4, y: 4, z: 4, core: 2. Of those that a mesh axis runs over, the one named last changes fastest.
Arguments:
- tokens: bfloat16 [512, 4096], P(('expert', 'dp')), may hold values from -6 to 6
- gate_weight: bfloat16 [4096, 28672], P(('expert', 'dp')), may hold values from -0.09375 to 0.09375
- up_weight: bfloat16 [4096, 28672], P(('expert', 'dp')), may hold values from -0.09375 to 0.09375
- down_weight_t: bfloat16 [4096, 28672], P(('expert', 'dp')), may hold values from -0.03125 to 0.03125
- router: bfloat16 [4096, 16], replicated, may hold values from -0.25 to 0.25
- cluster_ids: int32 [224], replicated, may hold values from 0 to 15, as said below
Outputs:
- residual: bfloat16 [512, 4096], P(('expert', 'dp'))
- grad_down: bfloat16 [4096, 28672], P(('expert', 'dp'))
The draws below stay inside these ranges and needn't reach their ends.
Inputs may be any that keep to these rules, and one draw needn't show every extreme that they name: `cluster_ids`: every expert holds one block or more. Experts e * 2 to e * 2 + 1 form group e; no group holds more than 64 blocks, and exactly one group holds that many.
All inputs are finite; a program needn't handle non-finite values.
Results may differ from the reference program's by a relative error of at most 0.0064.
Values may be sent and summed in bfloat16 or wider, within the bound.
A program may use at most 128 MiB of HBM per device.

```python
import jax
import jax.numpy as jnp
import numpy as np
from jax import lax

D = 4096
FF = 28672
BLOCK = 128
EXP_DEV = 2
NB = 224
EXPERTS = 16
TOKENS = 512
SLOTS = 4
N_DP = 16


def draw_cluster_ids(key, part):
    key = jax.random.fold_in(key, 11)
    group_total = EXPERTS // EXP_DEV
    heavy = SLOTS * N_DP
    others = NB - heavy
    shares = [1 + position % 3 for position in range(group_total - 1)]
    share_sum = sum(shares)
    group_sizes = [others * share // share_sum for share in shares]
    leftover = others - sum(group_sizes)
    for position in range(leftover):
        group_sizes[position] = group_sizes[position] + 1
    group_sizes = [heavy] + group_sizes
    member_sum = EXP_DEV * (EXP_DEV + 1) // 2
    labels = []
    for group_index in range(group_total):
        size_here = group_sizes[group_index]
        parts_here = [size_here * (member + 1) // member_sum for member in range(EXP_DEV)]
        parts_here[0] = parts_here[0] + size_here - sum(parts_here)
        for member in range(EXP_DEV):
            labels = labels + [group_index * EXP_DEV + member] * parts_here[member]
    static_labels = jnp.asarray(np.array(labels, dtype=np.int32))
    group_key, order_key = jax.random.split(key)
    ordering = jax.random.permutation(order_key, NB)
    shuffled = static_labels[ordering]
    relabel = jax.random.permutation(group_key, group_total).astype(jnp.int32)
    result = relabel[shuffled // EXP_DEV] * EXP_DEV + shuffled % EXP_DEV
    return result.astype(jnp.int32)


def block_scale(rng, dims, shards, least, top_value):
    def one(axis_at, blocks):
        steps = jax.random.uniform(jax.random.fold_in(jax.random.fold_in(rng, 6), axis_at), (blocks,), jnp.float32, least / len(shards), top_value / len(shards))
        return jnp.repeat(jnp.exp(steps), dims[axis_at] // blocks).reshape((-1,) + (1,) * (len(dims) - axis_at - 1))

    factor_of = one(*shards[0])
    for cut in shards[1:]:
        factor_of = factor_of * one(*cut)
    return factor_of


def bell_draw(own_key, dims, spread, limit, shards=(), kind=jnp.bfloat16):
    loudness = block_scale(own_key, dims, shards, -0.22, 0.18) if shards else 1.0
    values = jax.random.normal(own_key, dims, jnp.float32) * spread * loudness
    return jnp.minimum(jnp.maximum(values, -limit), limit).astype(kind)


def setup_inputs(seed: int = 0) -> dict:
    key_list = jax.random.split(jax.random.key(seed), 7)
    tokens = bell_draw(key_list[0], (TOKENS, D), 1.0, 6.0, ((0, 128),))
    gate_weight = bell_draw(key_list[1], (D, FF), D ** -0.5, 0.09375, ((0, 128),))
    up_weight = bell_draw(key_list[2], (D, FF), D ** -0.5, 0.09375, ((0, 128),))
    down_weight_t = bell_draw(key_list[3], (D, FF), FF ** -0.5, 0.03125, ((0, 128),))
    router = bell_draw(key_list[4], (D, EXPERTS), (D // 9) ** -0.5, 0.25)
    cluster_ids = draw_cluster_ids(jax.random.fold_in(key_list[6], 71), 0)
    return dict(tokens=tokens, gate_weight=gate_weight, up_weight=up_weight, down_weight_t=down_weight_t, router=router, cluster_ids=cluster_ids)


def reference(tokens, gate_weight, up_weight, down_weight_t, router, cluster_ids):
    gate_pre = jnp.dot(tokens, gate_weight, preferred_element_type=jnp.float32)
    up_pre = jnp.dot(tokens, up_weight, preferred_element_type=jnp.float32)
    hidden = jax.nn.silu(gate_pre) * up_pre
    logits = jnp.dot(tokens, router, preferred_element_type=jnp.float32)
    gate_scale = 2.0 * jax.nn.sigmoid(logits) - 1.0
    per_block = jnp.take(gate_scale, cluster_ids.astype(jnp.int32), axis=1)
    expanded = jnp.repeat(per_block, BLOCK, axis=1)
    scaled = (expanded * hidden).astype(jnp.bfloat16)
    residual_f = lax.dot_general(scaled, down_weight_t, (((1,), (1,)), ((), ())), preferred_element_type=jnp.float32)
    residual = residual_f.astype(jnp.bfloat16)
    grad_f = lax.dot_general(residual, scaled, (((0,), (0,)), ((), ())), preferred_element_type=jnp.float32)
    grad_down = (grad_f * (1.0 / math_sqrt(TOKENS))).astype(jnp.bfloat16)
    return (residual, grad_down)

def math_sqrt(value):
    return float(value) ** 0.5
```

```python
import jax
import jax.numpy as jnp
from jax import lax
from jax.experimental import pallas as pl
from jax.experimental.pallas import tpu as pltpu
from jax.sharding import PartitionSpec as P

MESH = pl.DeviceIdType.MESH
BF = jnp.bfloat16
F32 = jnp.float32

D = 4096
FF = 28672
EXPERTS = 16
BLOCK = 128
TOKENS = 512
NY = 4
ND = 16
ROWS = 32
KD = D // NY
FD = FF // ND
FC = FD // 2
CHUNKS = (2, 2, 3)
STARTS = (0, 2, 4)
H = 2
RH = ROWS // H
IH = ND * RH
TQ = TOKENS // NY
INV_ROOT = 1.0 / float(TOKENS) ** 0.5


def local_copy(src, dst, sem):
    return pltpu.make_async_copy(src, dst, sem)


def wait_bytes(ref, sem):
    pltpu.make_async_copy(ref, ref, sem).wait()


def kernel(
    tok, gw, uw, dw, router, ids,
    resid_out, grad_out,
    tok_send, tok_recv, tokens, wrecv, part, psum, logit, lsum, s, wd, p, rr, rfull, out16, gs,
    tok_s, w_s, w_r, p_s, p_r, l_s, l_r, s_s, s_r, d_s, d_r, rp_s, rp_r, ra_s, ra_r, o_s, o_r, g_s, g_r,
):
    e = lax.axis_index("expert")
    d = lax.axis_index("dp")
    y, c = e // 2, e % 2
    x, z = d // 4, d % 4

    def plane_peer(o):
        return ((x + o // 4) % 4) * 4 + (z + o % 4) % 4

    def remote(src, dst, ssem, rsem, te, td):
        pltpu.make_async_remote_copy(
            src, dst, ssem, rsem, device_id=(te, td), device_id_type=MESH
        ).start()

    def each(lo, hi, body):
        def step(o, carry):
            body(o)
            return carry

        lax.fori_loop(lo, hi, step, 0)

    bar = pltpu.get_barrier_semaphore()

    def greet_plane(o):
        pl.semaphore_signal(
            bar, inc=1, device_id=(y * 2 + (c + o % 2) % 2, plane_peer(o // 2)), device_id_type=MESH
        )

    each(1, 32, greet_plane)

    def greet_others(o):
        y2 = (y + 1 + o // 2) % 4
        pl.semaphore_signal(bar, inc=1, device_id=(y2 * 2 + o % 2, d), device_id_type=MESH)

    each(0, 6, greet_others)

    t = tok[...].astype(F32)
    t16 = jnp.concatenate([t] * 4, axis=0)
    row = lax.broadcasted_iota(jnp.int32, t16.shape, 0)
    t16 = jnp.where(row // 4 == y, t16, 0.0).astype(BF)
    for k in range(NY):
        tok_send[k] = t16[:, k * KD : (k + 1) * KD]

    pl.semaphore_wait(bar, 37)

    def send_tok_col(o):
        y2 = (y + o) % 4
        remote(tok_send.at[y2], tok_recv.at[o - 1], tok_s.at[0], tok_s.at[1], y2 * 2 + c, d)

    each(1, NY, send_tok_col)

    def issue_gu(m, k):
        w = (gw, uw)[m]
        n, first = CHUNKS[k], STARTS[k]
        me = c * ND + d

        def cols(c2, d2):
            return pl.ds(pl.multiple_of(d2 * FD + c2 * FC + first * BLOCK, BLOCK), n * BLOCK)

        def body(o):
            c2, d2 = (c + o % 2) % 2, plane_peer(o // 2)
            remote(w.at[:, cols(c2, d2)], wrecv[k].at[m, me], w_s.at[m, k], w_r.at[m, k], y * 2 + c2, d2)

        each(1, 32, body)
        local_copy(w.at[:, cols(c, d)], wrecv[k].at[m, me], w_r.at[m, k]).start()

    def issue_down(h):
        def cols(d2):
            return pl.ds(pl.multiple_of(d2 * FD, BLOCK), FD)

        rows = pl.ds(h * RH, RH)

        def body(o):
            d2 = plane_peer(o)
            remote(dw.at[rows, cols(d2)], wd.at[h, d], d_s.at[h], d_r.at[h], e, d2)

        each(1, ND, body)
        local_copy(dw.at[rows, cols(d)], wd.at[h, d], d_r.at[h]).start()

    issue_gu(0, 0)

    wait_bytes(tok_recv, tok_s.at[1])
    mine = tok_send[y].astype(F32)
    for k in range(NY - 1):
        mine = mine + tok_recv[k].astype(F32)
    tokens[d, c] = mine.astype(BF)

    def send_tok_plane(o):
        remote(tokens.at[d, c], tokens.at[d, c], tok_s.at[2], tok_s.at[3], e, plane_peer(o))

    each(1, ND, send_tok_plane)
    issue_gu(1, 0)
    issue_gu(0, 1)
    wait_bytes(tokens.at[pl.ds(0, ND - 1), 0], tok_s.at[3])
    remote(tokens.at[:, c], tokens.at[:, c], tok_s.at[4], tok_s.at[5], y * 2 + 1 - c, d)
    issue_gu(1, 1)
    wait_bytes(tokens.at[:, 0], tok_s.at[5])
    rows_all = tokens[...].reshape(TOKENS, KD)

    logit[...] = jnp.zeros_like(logit)
    logit[:, :EXPERTS] = jnp.dot(
        rows_all, router[pl.ds(pl.multiple_of(y * KD, KD), KD), :], preferred_element_type=F32
    )

    def rows_of(y2):
        return pl.ds(pl.multiple_of(y2 * TQ, TQ), TQ)

    def send_logit(o):
        y2 = (y + o) % 4
        remote(logit.at[rows_of(y2)], lsum.at[o - 1], l_s, l_r, y2 * 2 + c, d)

    each(1, NY, send_logit)

    def partial(k):
        n = CHUNKS[k]
        for m in range(2):
            wait_bytes(wrecv[k].at[m], w_r.at[m, k])
            got = wrecv[k][m].reshape(KD, n * BLOCK)
            part[k][m] = jnp.dot(rows_all, got, preferred_element_type=F32).astype(BF)

            def send(o):
                y2 = (y + o) % 4
                remote(part[k].at[m, rows_of(y2)], psum[k].at[m, o - 1], p_s.at[m, k], p_r.at[m, k], y2 * 2 + c, d)

            each(1, NY, send)

    def hidden(k):
        n, first = CHUNKS[k], STARTS[k]
        for m in range(2):
            wait_bytes(psum[k].at[m], p_r.at[m, k])
        sums = []
        for m in range(2):
            total = part[k][m, rows_of(y)].astype(F32)
            for o in range(NY - 1):
                total = total + psum[k][m, o].astype(F32)
            sums.append(total)
        lane = lax.broadcasted_iota(jnp.int32, (TQ, EXPERTS), 1)
        for j in range(n):
            expert = ids[d * (FD // BLOCK) + c * (FC // BLOCK) + first + j]
            scale = jnp.sum(jnp.where(lane == expert, gate_scale, 0.0), axis=1, keepdims=True)
            g = sums[0][:, j * BLOCK : (j + 1) * BLOCK]
            u = sums[1][:, j * BLOCK : (j + 1) * BLOCK]
            col = (first + j) * BLOCK
            s[c, rows_of(y), col : col + BLOCK] = (scale * (g * jax.nn.sigmoid(g) * u)).astype(BF)
        view = s.at[c, rows_of(y), pl.ds(first * BLOCK, n * BLOCK)]

        def send(o):
            remote(view, view, s_s.at[k], s_r.at[k], (e + o) % 8, d)

        each(1, 8, send)

    partial(0)
    issue_gu(0, 2)
    issue_gu(1, 2)
    partial(1)
    issue_down(0)

    wait_bytes(lsum, l_r)
    total = logit[rows_of(y), :EXPERTS]
    for o in range(NY - 1):
        total = total + lsum[o][:, :EXPERTS]
    gate_scale = 2.0 * jax.nn.sigmoid(total) - 1.0
    hidden(0)
    partial(2)
    issue_down(1)
    hidden(1)
    hidden(2)
    for k in range(3):
        wait_bytes(sview(s, k), s_r.at[k])

    def residual(h):
        wait_bytes(wd.at[h], d_r.at[h])
        w = wd[h].reshape(IH, FD)
        acc = lax.dot_general(s[0], w[:, :FC], (((1,), (1,)), ((), ())), preferred_element_type=F32)
        acc = acc + lax.dot_general(s[1], w[:, FC:], (((1,), (1,)), ((), ())), preferred_element_type=F32)
        p[h] = acc.astype(BF).reshape(ND, 32, IH)

        def send(o):
            d2 = plane_peer(o)
            remote(p.at[h, d2], rr.at[h, o - 1], rp_s.at[h], rp_r.at[h], e, d2)

        each(1, ND, send)

    def reduce_residual(h):
        wait_bytes(rr.at[h], rp_r.at[h])
        acc = p[h, d].astype(F32)
        for o in range(ND - 1):
            acc = acc + rr[h, o].astype(F32)
        rfull[h, d] = acc.astype(BF)
        view = rfull.at[h, d]

        def send(o):
            remote(view, view, ra_s.at[h], ra_r.at[h], e, plane_peer(o))

        each(1, ND, send)

        def send_out(o):
            e2 = (e + o) % 8
            rows = pl.ds(pl.multiple_of((e2 % 2) * 16, 16), 16)
            remote(rfull.at[h, d, rows], out16.at[e, h], o_s.at[h], o_r.at[h], e2, d)

        each(1, 8, send_out)
        rows = pl.ds(pl.multiple_of(c * 16, 16), 16)
        local_copy(rfull.at[h, d, rows], out16.at[e, h], o_r.at[h]).start()

    def gradient(h):
        wait_bytes(rfull.at[h, pl.ds(0, ND - 1)], ra_r.at[h])
        r = rfull[h].reshape(TOKENS, IH)
        for c2 in range(2):
            g = lax.dot_general(r, s[c2], (((0,), (0,)), ((), ())), preferred_element_type=F32)
            gs[h, :, :, c2 * FC : (c2 + 1) * FC] = (g * INV_ROOT).astype(BF).reshape(ND, RH, FC)
        rows = pl.ds(h * RH, RH)
        cols = pl.ds(pl.multiple_of(d * FD, BLOCK), FD)

        def send(o):
            d2 = plane_peer(o)
            remote(gs.at[h, d2], grad_out.at[rows, cols], g_s.at[h], g_r.at[h], e, d2)

        each(1, ND, send)
        local_copy(gs.at[h, d], grad_out.at[rows, cols], g_r.at[h]).start()

    residual(0)
    residual(1)
    reduce_residual(0)
    reduce_residual(1)
    gradient(0)
    gradient(1)

    for h in range(H):
        wait_bytes(out16.at[:, h], o_r.at[h])
    both = jnp.concatenate([out16[:, h].reshape(8 * 16, IH) for h in range(H)], axis=1)
    src = lax.broadcasted_iota(jnp.int32, (H * IH, H * IH), 0)
    dst = lax.broadcasted_iota(jnp.int32, (H * IH, H * IH), 1)
    place = (dst // ROWS) * RH + ((dst % ROWS) // RH) * IH + dst % RH
    order = jnp.where(src == place, 1.0, 0.0).astype(BF)
    ordered = jnp.dot(both, order, preferred_element_type=F32)
    for k in range(8):
        rows16 = ordered[k * 16 : (k + 1) * 16]
        pick = jnp.where(y == 0, rows16[0:4], 0.0)
        for y2 in range(1, NY):
            pick = jnp.where(y == y2, rows16[4 * y2 : 4 * y2 + 4], pick)
        resid_out[:, k * H * IH : (k + 1) * H * IH] = pick.astype(BF)

    wait_bytes(tok_recv, tok_s.at[0])
    wait_bytes(tokens.at[pl.ds(0, ND - 1), 0], tok_s.at[2])
    wait_bytes(tokens.at[:, 0], tok_s.at[4])
    wait_bytes(lsum, l_s)
    for k in range(3):
        for m in range(2):
            wait_bytes(wrecv[k].at[m, pl.ds(0, 31)], w_s.at[m, k])
            wait_bytes(psum[k].at[m], p_s.at[m, k])
        wait_bytes(sview(s, k), s_s.at[k])
    for h in range(H):
        wait_bytes(wd.at[h, pl.ds(0, ND - 1)], d_s.at[h])
        wait_bytes(rr.at[h], rp_s.at[h])
        wait_bytes(rfull.at[h, pl.ds(0, ND - 1)], ra_s.at[h])
        wait_bytes(out16.at[pl.ds(0, 7), h], o_s.at[h])
        wait_bytes(gs.at[h, pl.ds(0, ND - 1)], g_s.at[h])
        wait_bytes(grad_out.at[pl.ds(h * RH, RH)], g_r.at[h])


def sview(s, k):
    return s.at[0, pl.ds(0, 7 * 64), pl.ds(0, 2 * CHUNKS[k] * BLOCK)]


def per_device(tokens, gate_weight, up_weight, down_weight_t, router, cluster_ids):
    dma = pltpu.SemaphoreType.DMA
    nk = len(CHUNKS)
    hbm = pl.BlockSpec(memory_space=pl.ANY)
    vmem = pl.BlockSpec(memory_space=pltpu.VMEM)
    smem = pl.BlockSpec(memory_space=pltpu.SMEM)
    return pl.pallas_call(
        kernel,
        out_shape=(
            jax.ShapeDtypeStruct((TOKENS // 128, D), BF),
            jax.ShapeDtypeStruct((ROWS, FF), BF),
        ),
        in_specs=[vmem, hbm, hbm, hbm, vmem, smem],
        out_specs=(vmem, hbm),
        scratch_shapes=[
            pltpu.VMEM((NY, 16, KD), BF),
            pltpu.VMEM((NY - 1, 16, KD), BF),
            pltpu.VMEM((ND, 2, 16, KD), BF),
            tuple(pltpu.VMEM((2, 32, ROWS, n * BLOCK), BF) for n in CHUNKS),
            tuple(pltpu.VMEM((2, TOKENS, n * BLOCK), BF) for n in CHUNKS),
            tuple(pltpu.VMEM((2, NY - 1, TQ, n * BLOCK), BF) for n in CHUNKS),
            pltpu.VMEM((TOKENS, 128), F32),
            pltpu.VMEM((NY - 1, TQ, 128), F32),
            pltpu.VMEM((2, TOKENS, FC), BF),
            pltpu.VMEM((H, ND, RH, FD), BF),
            pltpu.VMEM((H, ND, 32, IH), BF),
            pltpu.VMEM((H, ND - 1, 32, IH), BF),
            pltpu.VMEM((H, ND, 32, IH), BF),
            pltpu.VMEM((8, H, 16, IH), BF),
            pltpu.VMEM((H, ND, RH, FD), BF),
            dma((6,)),
            dma((2, nk)), dma((2, nk)),
            dma((2, nk)), dma((2, nk)),
            dma, dma,
            dma((nk,)), dma((nk,)),
            dma((H,)), dma((H,)),
            dma((H,)), dma((H,)),
            dma((H,)), dma((H,)),
            dma((H,)), dma((H,)),
            dma((H,)), dma((H,)),
        ],
        compiler_params=pltpu.CompilerParams(
            collective_id=0, has_side_effects=True, vmem_limit_bytes=48 * 2**20
        ),
    )(tokens, gate_weight, up_weight, down_weight_t, router, cluster_ids)


def solution(mesh):
    split = P(("expert", "dp"), None)
    return jax.shard_map(
        per_device,
        mesh=mesh,
        in_specs=(split, split, split, split, P(), P()),
        out_specs=(split, split),
        check_vma=False,
    )
```

```python
import jax
import jax.numpy as jnp
from jax import lax
from jax.experimental import pallas as pl
from jax.experimental.pallas import tpu as pltpu
from jax.sharding import PartitionSpec as P

MESH = pl.DeviceIdType.MESH
BF = jnp.bfloat16
F32 = jnp.float32

D = 4096
FF = 28672
EXPERTS = 16
BLOCK = 128
TOKENS = 512
NY = 4
ND = 16
ROWS = 32
KD = D // NY
FD = FF // ND
FC = FD // 2
CHUNKS = (2, 2, 2, 1)
STARTS = (0, 2, 4, 6)
NK = len(CHUNKS)
SENT = ((F32, BF), (F32, BF), (F32, BF), (F32, BF))
H = 2
RH = ROWS // H
IH = ND * RH
TQ = TOKENS // NY
PLAN = (
    ("I", 0, 2), ("I", 1, 2), ("P", 0, 0), ("P", 1, 0), ("I", 0, 3), ("I", 1, 3), ("D", 0), ("D", 1), ("L",),
    ("P", 0, 1), ("P", 1, 1), ("H", 0), ("P", 0, 2), ("P", 1, 2), ("H", 1), ("F", 0),
    ("P", 0, 3), ("P", 1, 3), ("H", 2), ("F", 1), ("H", 3), ("F", 2), ("F", 3),
)
INV_ROOT = 1.0 / float(TOKENS) ** 0.5


def local_copy(src, dst, sem):
    return pltpu.make_async_copy(src, dst, sem)


def wait_bytes(ref, sem):
    pltpu.make_async_copy(ref, ref, sem).wait()


def kernel(
    tok_in, gw, uw, dw, router_in, ids,
    resid_out, grad_out,
    tok, router, tok_send, tok_recv, tokens, wrecv, part, own, psum, logit, lsum, s, wd, p, rr, rfull, out16, gs,
    in_s, tok_s, w_s, w_r, p_s, p_r, l_s, l_r, s_s, s_r, f_s, f_r, d_s, d_r, rp_s, rp_r, ra_s, ra_r, o_s, o_r, g_s, g_r,
):
    e = lax.axis_index("expert")
    d = lax.axis_index("dp")
    y, c = e // 2, e % 2
    x, z = d // 4, d % 4

    def plane_peer(o):
        return ((x + o // 4) % 4) * 4 + (z + o % 4) % 4

    def remote(src, dst, ssem, rsem, te, td):
        pltpu.make_async_remote_copy(
            src, dst, ssem, rsem, device_id=(te, td), device_id_type=MESH
        ).start()

    def each(lo, hi, body):
        def step(o, carry):
            body(o)
            return carry

        lax.fori_loop(lo, hi, step, 0)

    tok_copy = local_copy(tok_in, tok, in_s.at[0])
    tok_copy.start()
    router_copy = local_copy(
        router_in.at[:, pl.ds(pl.multiple_of(y * KD, KD), KD)], router, in_s.at[1]
    )
    router_copy.start()

    bar = pltpu.get_barrier_semaphore()

    def greet_plane(o):
        pl.semaphore_signal(
            bar, inc=1, device_id=(y * 2 + (c + o % 2) % 2, plane_peer(o // 2)), device_id_type=MESH
        )

    each(1, 32, greet_plane)

    def greet_others(o):
        y2 = (y + 1 + o // 2) % 4
        pl.semaphore_signal(bar, inc=1, device_id=(y2 * 2 + o % 2, d), device_id_type=MESH)

    each(0, 6, greet_others)

    tok_copy.wait()
    t = tok[...].astype(F32)
    t16 = jnp.concatenate([t] * 4, axis=0)
    row = lax.broadcasted_iota(jnp.int32, t16.shape, 0)
    t16 = jnp.where(row // 4 == y, t16, 0.0).astype(BF)
    for k in range(NY):
        tok_send[k] = t16[:, k * KD : (k + 1) * KD]

    pl.semaphore_wait(bar, 37)

    def send_tok_col(o):
        y2 = (y + o) % 4
        remote(tok_send.at[y2], tok_recv.at[o - 1], tok_s.at[0], tok_s.at[1], y2 * 2 + c, d)

    each(1, NY, send_tok_col)

    def issue_gu(m, k):
        w = (gw, uw)[m]
        n, first = CHUNKS[k], STARTS[k]
        me = c * ND + d

        def cols(c2, d2):
            return pl.ds(pl.multiple_of(d2 * FD + c2 * FC + first * BLOCK, BLOCK), n * BLOCK)

        def body(o):
            c2, d2 = (c + o % 2) % 2, plane_peer(o // 2)
            remote(w.at[:, cols(c2, d2)], wrecv[k].at[m, me], w_s.at[m, k], w_r.at[m, k], y * 2 + c2, d2)

        each(1, 32, body)
        local_copy(w.at[:, cols(c, d)], wrecv[k].at[m, me], w_r.at[m, k]).start()

    def issue_down(h):
        def cols(d2):
            return pl.ds(pl.multiple_of(d2 * FD, BLOCK), FD)

        rows = pl.ds(h * RH, RH)

        def body(o):
            d2 = plane_peer(o)
            remote(dw.at[rows, cols(d2)], wd.at[h, d], d_s.at[h], d_r.at[h], e, d2)

        each(1, ND, body)
        local_copy(dw.at[rows, cols(d)], wd.at[h, d], d_r.at[h]).start()

    issue_gu(0, 0)

    wait_bytes(tok_recv, tok_s.at[1])
    mine = tok_send[y].astype(F32)
    for k in range(NY - 1):
        mine = mine + tok_recv[k].astype(F32)
    tokens[d, c] = mine.astype(BF)

    def send_tok_plane(o):
        remote(tokens.at[d, c], tokens.at[d, c], tok_s.at[2], tok_s.at[3], e, plane_peer(o))

    each(1, ND, send_tok_plane)
    issue_gu(1, 0)
    issue_gu(0, 1)
    wait_bytes(tokens.at[pl.ds(0, ND - 1), 0], tok_s.at[3])
    remote(tokens.at[:, c], tokens.at[:, c], tok_s.at[4], tok_s.at[5], y * 2 + 1 - c, d)
    issue_gu(1, 1)
    wait_bytes(tokens.at[:, 0], tok_s.at[5])
    rows_all = tokens[...].reshape(TOKENS, KD)

    router_copy.wait()
    logit[...] = jnp.zeros_like(logit)
    logit[:, :EXPERTS] = lax.dot_general(
        rows_all, router[...], (((1,), (1,)), ((), ())), preferred_element_type=F32
    )

    def rows_of(y2):
        return pl.ds(pl.multiple_of(y2 * TQ, TQ), TQ)

    def send_logit(o):
        y2 = (y + o) % 4
        remote(logit.at[rows_of(y2)], lsum.at[o - 1], l_s, l_r, y2 * 2 + c, d)

    each(1, NY, send_logit)

    def partial(m, k):
        n = CHUNKS[k]
        wait_bytes(wrecv[k].at[m], w_r.at[m, k])
        got = wrecv[k][m].reshape(KD, n * BLOCK)
        dot = jnp.dot(rows_all, got, preferred_element_type=F32)
        if SENT[k][m] == F32:
            part[k][m][...] = dot
        else:
            part[k][m][...] = dot.astype(BF)
            own[k][m][...] = dot

        def send(o):
            y2 = (y + o) % 4
            remote(part[k][m].at[rows_of(y2)], psum[k][m].at[o - 1], p_s.at[m, k], p_r.at[m, k], y2 * 2 + c, d)

        each(1, NY, send)

    def step_cols(k):
        return pl.ds(STARTS[k] * BLOCK, CHUNKS[k] * BLOCK)

    def hidden(k):
        n, first = CHUNKS[k], STARTS[k]
        sums = []
        for m in range(2):
            wait_bytes(psum[k][m], p_r.at[m, k])
            kept = part[k][m] if SENT[k][m] == F32 else own[k][m]
            total = kept[rows_of(y)]
            for o in range(NY - 1):
                total = total + psum[k][m][o].astype(F32)
            sums.append(total)
        lane = lax.broadcasted_iota(jnp.int32, (TQ, EXPERTS), 1)
        for j in range(n):
            expert = ids[d * (FD // BLOCK) + c * (FC // BLOCK) + first + j]
            scale = jnp.sum(jnp.where(lane == expert, gate_scale, 0.0), axis=1, keepdims=True)
            g = sums[0][:, j * BLOCK : (j + 1) * BLOCK]
            u = sums[1][:, j * BLOCK : (j + 1) * BLOCK]
            col = (first + j) * BLOCK
            s[c, rows_of(y), col : col + BLOCK] = (scale * (g * jax.nn.sigmoid(g) * u)).astype(BF)
        view = s.at[c, rows_of(y), step_cols(k)]

        def send(o):
            remote(view, view, s_s.at[k], s_r.at[k], (y + o) % 4 * 2 + c, d)

        each(1, NY, send)

    def hand_over(k):
        wait_bytes(s.at[0, pl.ds(0, 3 * TQ), step_cols(k)], s_r.at[k])
        view = s.at[c, :, step_cols(k)]
        remote(view, view, f_s.at[k], f_r.at[k], y * 2 + 1 - c, d)

    for op in PLAN:
        if op[0] == "I":
            issue_gu(*op[1:])
        elif op[0] == "D":
            issue_down(op[1])
        elif op[0] == "P":
            partial(*op[1:])
        elif op[0] == "L":
            wait_bytes(lsum, l_r)
            total = logit[rows_of(y), :EXPERTS]
            for o in range(NY - 1):
                total = total + lsum[o][:, :EXPERTS]
            gate_scale = 2.0 * jax.nn.sigmoid(total) - 1.0
        elif op[0] == "H":
            hidden(op[1])
        else:
            hand_over(op[1])
    for k in range(NK):
        wait_bytes(s.at[0, :, step_cols(k)], f_r.at[k])

    def residual(h):
        wait_bytes(wd.at[h], d_r.at[h])
        w = wd[h].reshape(IH, FD)
        acc = lax.dot_general(s[0], w[:, :FC], (((1,), (1,)), ((), ())), preferred_element_type=F32)
        acc = acc + lax.dot_general(s[1], w[:, FC:], (((1,), (1,)), ((), ())), preferred_element_type=F32)
        p[h] = acc.astype(BF).reshape(ND, 32, IH)

        def send(o):
            d2 = plane_peer(o)
            remote(p.at[h, d2], rr.at[h, o - 1], rp_s.at[h], rp_r.at[h], e, d2)

        each(1, ND, send)

    def reduce_residual(h):
        wait_bytes(rr.at[h], rp_r.at[h])
        acc = p[h, d].astype(F32)
        for o in range(ND - 1):
            acc = acc + rr[h, o].astype(F32)
        rfull[h, d] = acc.astype(BF)
        view = rfull.at[h, d]

        def send(o):
            remote(view, view, ra_s.at[h], ra_r.at[h], e, plane_peer(o))

        each(1, ND, send)

        def send_out(o):
            e2 = (e + o) % 8
            rows = pl.ds(pl.multiple_of((e2 % 2) * 16, 16), 16)
            remote(rfull.at[h, d, rows], out16.at[e, h], o_s.at[h], o_r.at[h], e2, d)

        each(1, 8, send_out)
        rows = pl.ds(pl.multiple_of(c * 16, 16), 16)
        local_copy(rfull.at[h, d, rows], out16.at[e, h], o_r.at[h]).start()

    def gradient(h):
        wait_bytes(rfull.at[h, pl.ds(0, ND - 1)], ra_r.at[h])
        r = rfull[h].reshape(TOKENS, IH)
        for c2 in range(2):
            g = lax.dot_general(r, s[c2], (((0,), (0,)), ((), ())), preferred_element_type=F32)
            gs[h, :, :, c2 * FC : (c2 + 1) * FC] = (g * INV_ROOT).astype(BF).reshape(ND, RH, FC)
        rows = pl.ds(h * RH, RH)
        cols = pl.ds(pl.multiple_of(d * FD, BLOCK), FD)

        def send(o):
            d2 = plane_peer(o)
            remote(gs.at[h, d2], grad_out.at[rows, cols], g_s.at[h], g_r.at[h], e, d2)

        each(1, ND, send)
        local_copy(gs.at[h, d], grad_out.at[rows, cols], g_r.at[h]).start()

    residual(0)
    residual(1)
    reduce_residual(0)
    reduce_residual(1)
    gradient(0)
    gradient(1)

    for h in range(H):
        wait_bytes(out16.at[:, h], o_r.at[h])
    both = jnp.concatenate([out16[:, h].reshape(8 * 16, IH) for h in range(H)], axis=1)
    src = lax.broadcasted_iota(jnp.int32, (H * IH, H * IH), 0)
    dst = lax.broadcasted_iota(jnp.int32, (H * IH, H * IH), 1)
    place = (dst // ROWS) * RH + ((dst % ROWS) // RH) * IH + dst % RH
    order = jnp.where(src == place, 1.0, 0.0).astype(BF)
    ordered = jnp.dot(both, order, preferred_element_type=F32)
    for k in range(8):
        rows16 = ordered[k * 16 : (k + 1) * 16]
        pick = jnp.where(y == 0, rows16[0:4], 0.0)
        for y2 in range(1, NY):
            pick = jnp.where(y == y2, rows16[4 * y2 : 4 * y2 + 4], pick)
        resid_out[:, k * H * IH : (k + 1) * H * IH] = pick.astype(BF)

    wait_bytes(tok_recv, tok_s.at[0])
    wait_bytes(tokens.at[pl.ds(0, ND - 1), 0], tok_s.at[2])
    wait_bytes(tokens.at[:, 0], tok_s.at[4])
    wait_bytes(lsum, l_s)
    for k in range(NK):
        for m in range(2):
            wait_bytes(wrecv[k].at[m, pl.ds(0, 31)], w_s.at[m, k])
            wait_bytes(psum[k][m], p_s.at[m, k])
        wait_bytes(s.at[0, pl.ds(0, 3 * TQ), step_cols(k)], s_s.at[k])
        wait_bytes(s.at[0, :, step_cols(k)], f_s.at[k])
    for h in range(H):
        wait_bytes(wd.at[h, pl.ds(0, ND - 1)], d_s.at[h])
        wait_bytes(rr.at[h], rp_s.at[h])
        wait_bytes(rfull.at[h, pl.ds(0, ND - 1)], ra_s.at[h])
        wait_bytes(out16.at[pl.ds(0, 7), h], o_s.at[h])
        wait_bytes(gs.at[h, pl.ds(0, ND - 1)], g_s.at[h])
        wait_bytes(grad_out.at[pl.ds(h * RH, RH)], g_r.at[h])


def per_device(tokens, gate_weight, up_weight, down_weight_t, router, cluster_ids):
    dma = pltpu.SemaphoreType.DMA
    nk = NK
    hbm = pl.BlockSpec(memory_space=pltpu.HBM)
    vmem = pl.BlockSpec(memory_space=pltpu.VMEM)
    smem = pl.BlockSpec(memory_space=pltpu.SMEM)
    return pl.pallas_call(
        kernel,
        out_shape=(
            jax.ShapeDtypeStruct((TOKENS // 128, D), BF),
            jax.ShapeDtypeStruct((ROWS, FF), BF),
        ),
        in_specs=[hbm, hbm, hbm, hbm, hbm, smem],
        out_specs=(vmem, pl.BlockSpec(memory_space=pl.ANY)),
        scratch_shapes=[
            pltpu.VMEM((TOKENS // 128, D), BF),
            pltpu.VMEM((EXPERTS, KD), BF),
            pltpu.VMEM((NY, 16, KD), BF),
            pltpu.VMEM((NY - 1, 16, KD), BF),
            pltpu.VMEM((ND, 2, 16, KD), BF),
            tuple(pltpu.VMEM((2, 32, ROWS, n * BLOCK), BF) for n in CHUNKS),
            tuple(tuple(pltpu.VMEM((TOKENS, n * BLOCK), t) for t in ts) for n, ts in zip(CHUNKS, SENT)),
            tuple(tuple(pltpu.VMEM((TOKENS, n * BLOCK), F32) for _ in range(2)) for n in CHUNKS),
            tuple(tuple(pltpu.VMEM((NY - 1, TQ, n * BLOCK), t) for t in ts) for n, ts in zip(CHUNKS, SENT)),
            pltpu.VMEM((TOKENS, 128), F32),
            pltpu.VMEM((NY - 1, TQ, 128), F32),
            pltpu.VMEM((2, TOKENS, FC), BF),
            pltpu.VMEM((H, ND, RH, FD), BF),
            pltpu.VMEM((H, ND, 32, IH), BF),
            pltpu.VMEM((H, ND - 1, 32, IH), BF),
            pltpu.VMEM((H, ND, 32, IH), BF),
            pltpu.VMEM((8, H, 16, IH), BF),
            pltpu.VMEM((H, ND, RH, FD), BF),
            dma((2,)),
            dma((6,)),
            dma((2, nk)), dma((2, nk)),
            dma((2, nk)), dma((2, nk)),
            dma, dma,
            dma((nk,)), dma((nk,)),
            dma((nk,)), dma((nk,)),
            dma((H,)), dma((H,)),
            dma((H,)), dma((H,)),
            dma((H,)), dma((H,)),
            dma((H,)), dma((H,)),
            dma((H,)), dma((H,)),
        ],
        compiler_params=pltpu.CompilerParams(
            collective_id=0, has_side_effects=True, vmem_limit_bytes=54 * 2**20
        ),
    )(tokens, gate_weight, up_weight, down_weight_t, router.T, cluster_ids)


def solution(mesh):
    split = P(("expert", "dp"), None)
    return jax.shard_map(
        per_device,
        mesh=mesh,
        in_specs=(split, split, split, split, P(), P()),
        out_specs=(split, split),
        check_vma=False,
    )
```

```python
import jax
import jax.numpy as jnp
from jax import lax
from jax.experimental import pallas as pl
from jax.experimental.pallas import tpu as pltpu
from jax.sharding import PartitionSpec as P

MESH = pl.DeviceIdType.MESH
BF = jnp.bfloat16
F32 = jnp.float32

D = 4096
FF = 28672
EXPERTS = 16
BLOCK = 128
TOKENS = 512
NY = 4
ND = 16
ROWS = 32
KD = D // NY
FD = FF // ND
FC = FD // 2
CHUNKS = (2, 2, 2, 1)
STARTS = (0, 2, 4, 6)
NK = len(CHUNKS)
SENT = ((F32, BF), (F32, BF), (F32, BF), (F32, BF))
H = 2
RH = ROWS // H
IH = ND * RH
TQ = TOKENS // NY
PLAN = (
    ("I", 0, 2), ("I", 1, 2), ("P", 0, 0), ("P", 1, 0), ("I", 0, 3), ("I", 1, 3), ("D", 0), ("D", 1), ("L",),
    ("P", 0, 1), ("P", 1, 1), ("H", 0), ("P", 0, 2), ("P", 1, 2), ("H", 1), ("F", 0),
    ("P", 0, 3), ("P", 1, 3), ("H", 2), ("F", 1), ("H", 3), ("F", 2), ("F", 3),
)
DOWN_CUTS = (((0, 896), (896, 896)), ((0, 896), (896, 896)))
GRAD_CUTS = (((0, 896),), ((0, 896),))
INV_ROOT = 1.0 / float(TOKENS) ** 0.5


def div(a, b):
    return lax.div(a, jnp.int32(b))


def rem(a, b):
    return lax.rem(a, jnp.int32(b))


def local_copy(src, dst, sem):
    return pltpu.make_async_copy(src, dst, sem)


def wait_bytes(ref, sem):
    pltpu.make_async_copy(ref, ref, sem).wait()


def kernel(
    tok_in, gw, uw, dw, router_in, ids,
    resid_out, grad_out,
    tok, router, tok_send, tok_recv, tokens, wrecv, part, own, psum, logit, lsum, s, wd, p, rr, rfull, out16, gs,
    in_s, tok_s, w_s, w_r, p_s, p_r, l_s, l_r, s_s, s_r, f_s, f_r, d_s, d_r, rp_s, rp_r, ra_s, ra_r, o_s, o_r, g_s, g_r,
):
    e = lax.axis_index("expert")
    d = lax.axis_index("dp")
    y, c = div(e, 2), rem(e, 2)
    x, z = div(d, 4), rem(d, 4)

    def plane_peer(o):
        return rem(x + div(o, 4), 4) * 4 + rem(z + rem(o, 4), 4)

    def remote(src, dst, ssem, rsem, te, td):
        pltpu.make_async_remote_copy(
            src, dst, ssem, rsem, device_id=(te, td), device_id_type=MESH
        ).start()

    def each(lo, hi, body):
        def step(o, carry):
            body(o)
            return carry

        lax.fori_loop(lo, hi, step, 0)

    tok_copy = local_copy(tok_in, tok, in_s.at[0])
    tok_copy.start()
    router_copy = local_copy(
        router_in.at[:, pl.ds(pl.multiple_of(y * KD, KD), KD)], router, in_s.at[1]
    )
    router_copy.start()

    bar = pltpu.get_barrier_semaphore()

    def greet_plane(o):
        pl.semaphore_signal(
            bar, inc=1, device_id=(y * 2 + rem(c + rem(o, 2), 2), plane_peer(div(o, 2))), device_id_type=MESH
        )

    each(1, 32, greet_plane)

    def greet_others(o):
        y2 = rem(y + 1 + div(o, 2), 4)
        pl.semaphore_signal(bar, inc=1, device_id=(y2 * 2 + rem(o, 2), d), device_id_type=MESH)

    each(0, 6, greet_others)

    pl.semaphore_wait(bar, 37)

    def issue_gu(m, k):
        w = (gw, uw)[m]
        n, first = CHUNKS[k], STARTS[k]
        me = c * ND + d

        def cols(c2, d2):
            return pl.ds(pl.multiple_of(d2 * FD + c2 * FC + first * BLOCK, BLOCK), n * BLOCK)

        def body(o):
            c2, d2 = rem(c + rem(o, 2), 2), plane_peer(div(o, 2))
            remote(w.at[:, cols(c2, d2)], wrecv[k].at[m, me], w_s.at[m, k], w_r.at[m, k], y * 2 + c2, d2)

        each(1, 32, body)
        local_copy(w.at[:, cols(c, d)], wrecv[k].at[m, me], w_r.at[m, k]).start()

    def issue_down(h):
        rows = pl.ds(h * RH, RH)
        for first, width in DOWN_CUTS[h]:

            def cols(d2):
                return pl.ds(pl.multiple_of(d2 * FD + first, BLOCK), width)

            to = wd.at[h, d, :, pl.ds(first, width)]

            def body(o):
                d2 = plane_peer(o)
                remote(dw.at[rows, cols(d2)], to, d_s.at[h], d_r.at[h], e, d2)

            each(1, ND, body)
            local_copy(dw.at[rows, cols(d)], to, d_r.at[h]).start()

    issue_gu(0, 0)

    tok_copy.wait()
    t = tok[...].astype(F32)
    t16 = jnp.concatenate([t] * 4, axis=0)
    row = lax.broadcasted_iota(jnp.int32, t16.shape, 0)
    t16 = jnp.where(row // 4 == y, t16, 0.0).astype(BF)
    for k in range(NY):
        tok_send[k] = t16[:, k * KD : (k + 1) * KD]

    def send_tok_col(o):
        y2 = rem(y + o, 4)
        remote(tok_send.at[y2], tok_recv.at[o - 1], tok_s.at[0], tok_s.at[1], y2 * 2 + c, d)

    each(1, NY, send_tok_col)

    wait_bytes(tok_recv, tok_s.at[1])
    mine = tok_send[y].astype(F32)
    for k in range(NY - 1):
        mine = mine + tok_recv[k].astype(F32)
    tokens[d, c] = mine.astype(BF)

    def send_tok_plane(o):
        remote(tokens.at[d, c], tokens.at[d, c], tok_s.at[2], tok_s.at[3], e, plane_peer(o))

    each(1, ND, send_tok_plane)
    issue_gu(1, 0)
    issue_gu(0, 1)
    wait_bytes(tokens.at[pl.ds(0, ND - 1), 0], tok_s.at[3])
    remote(tokens.at[:, c], tokens.at[:, c], tok_s.at[4], tok_s.at[5], y * 2 + 1 - c, d)
    issue_gu(1, 1)
    wait_bytes(tokens.at[:, 0], tok_s.at[5])
    rows_all = tokens[...].reshape(TOKENS, KD)

    router_copy.wait()
    logit[...] = jnp.zeros_like(logit)
    logit[:, :EXPERTS] = lax.dot_general(
        rows_all, router[...], (((1,), (1,)), ((), ())), preferred_element_type=F32
    )

    def rows_of(y2):
        return pl.ds(pl.multiple_of(y2 * TQ, TQ), TQ)

    def send_logit(o):
        y2 = rem(y + o, 4)
        remote(logit.at[rows_of(y2)], lsum.at[o - 1], l_s, l_r, y2 * 2 + c, d)

    each(1, NY, send_logit)

    def partial(m, k):
        n = CHUNKS[k]
        wait_bytes(wrecv[k].at[m], w_r.at[m, k])
        got = wrecv[k][m].reshape(KD, n * BLOCK)
        dot = jnp.dot(rows_all, got, preferred_element_type=F32)
        if SENT[k][m] == F32:
            part[k][m][...] = dot
        else:
            part[k][m][...] = dot.astype(BF)
            own[k][m][...] = dot

        def send(o):
            y2 = rem(y + o, 4)
            remote(part[k][m].at[rows_of(y2)], psum[k][m].at[o - 1], p_s.at[m, k], p_r.at[m, k], y2 * 2 + c, d)

        each(1, NY, send)

    def step_cols(k):
        return pl.ds(STARTS[k] * BLOCK, CHUNKS[k] * BLOCK)

    def hidden(k):
        n, first = CHUNKS[k], STARTS[k]
        sums = []
        for m in range(2):
            wait_bytes(psum[k][m], p_r.at[m, k])
            kept = part[k][m] if SENT[k][m] == F32 else own[k][m]
            total = kept[rows_of(y)]
            for o in range(NY - 1):
                total = total + psum[k][m][o].astype(F32)
            sums.append(total)
        lane = lax.broadcasted_iota(jnp.int32, (TQ, EXPERTS), 1)
        for j in range(n):
            expert = ids[d * (FD // BLOCK) + c * (FC // BLOCK) + first + j]
            scale = jnp.sum(jnp.where(lane == expert, gate_scale, 0.0), axis=1, keepdims=True)
            g = sums[0][:, j * BLOCK : (j + 1) * BLOCK]
            u = sums[1][:, j * BLOCK : (j + 1) * BLOCK]
            col = (first + j) * BLOCK
            s[c, rows_of(y), col : col + BLOCK] = (scale * (g * jax.nn.sigmoid(g) * u)).astype(BF)
        view = s.at[c, rows_of(y), step_cols(k)]

        def send(o):
            remote(view, view, s_s.at[k], s_r.at[k], rem(y + o, 4) * 2 + c, d)

        each(1, NY, send)

    def hand_over(k):
        wait_bytes(s.at[0, pl.ds(0, 3 * TQ), step_cols(k)], s_r.at[k])
        view = s.at[c, :, step_cols(k)]
        remote(view, view, f_s.at[k], f_r.at[k], y * 2 + 1 - c, d)

    for op in PLAN:
        if op[0] == "I":
            issue_gu(*op[1:])
        elif op[0] == "D":
            issue_down(op[1])
        elif op[0] == "P":
            partial(*op[1:])
        elif op[0] == "L":
            wait_bytes(lsum, l_r)
            total = logit[rows_of(y), :EXPERTS]
            for o in range(NY - 1):
                total = total + lsum[o][:, :EXPERTS]
            gate_scale = 2.0 * jax.nn.sigmoid(total) - 1.0
        elif op[0] == "H":
            hidden(op[1])
        else:
            hand_over(op[1])
    for k in range(NK):
        wait_bytes(s.at[0, :, step_cols(k)], f_r.at[k])

    def residual(h):
        wait_bytes(wd.at[h], d_r.at[h])
        w = wd[h].reshape(IH, FD)
        acc = lax.dot_general(s[0], w[:, :FC], (((1,), (1,)), ((), ())), preferred_element_type=F32)
        acc = acc + lax.dot_general(s[1], w[:, FC:], (((1,), (1,)), ((), ())), preferred_element_type=F32)
        p[h] = acc.astype(BF).reshape(ND, 32, IH)

        def send(o):
            d2 = plane_peer(o)
            remote(p.at[h, d2], rr.at[h, o - 1], rp_s.at[h], rp_r.at[h], e, d2)

        each(1, ND, send)

    def reduce_residual(h):
        wait_bytes(rr.at[h], rp_r.at[h])
        acc = p[h, d].astype(F32)
        for o in range(ND - 1):
            acc = acc + rr[h, o].astype(F32)
        rfull[h, d] = acc.astype(BF)
        view = rfull.at[h, d]

        def send(o):
            remote(view, view, ra_s.at[h], ra_r.at[h], e, plane_peer(o))

        each(1, ND, send)

        def send_out(o):
            e2 = rem(e + o, 8)
            rows = pl.ds(pl.multiple_of(rem(e2, 2) * 16, 16), 16)
            remote(rfull.at[h, d, rows], out16.at[e, h], o_s.at[h], o_r.at[h], e2, d)

        each(1, 8, send_out)
        rows = pl.ds(pl.multiple_of(c * 16, 16), 16)
        local_copy(rfull.at[h, d, rows], out16.at[e, h], o_r.at[h]).start()

    def gradient(h):
        wait_bytes(rfull.at[h, pl.ds(0, ND - 1)], ra_r.at[h])
        r = rfull[h].reshape(TOKENS, IH)
        rows = pl.ds(h * RH, RH)
        for c2 in range(2):
            g = lax.dot_general(r, s[c2], (((0,), (0,)), ((), ())), preferred_element_type=F32)
            gs[h, :, :, c2 * FC : (c2 + 1) * FC] = (g * INV_ROOT).astype(BF).reshape(ND, RH, FC)
            for first, width in GRAD_CUTS[h]:
                cols = pl.ds(pl.multiple_of(d * FD + c2 * FC + first, BLOCK), width)
                part_cols = pl.ds(c2 * FC + first, width)

                def send(o):
                    d2 = plane_peer(o)
                    remote(gs.at[h, d2, :, part_cols], grad_out.at[rows, cols], g_s.at[h], g_r.at[h], e, d2)

                each(1, ND, send)
                local_copy(gs.at[h, d, :, part_cols], grad_out.at[rows, cols], g_r.at[h]).start()

    residual(0)
    residual(1)
    reduce_residual(0)
    reduce_residual(1)
    gradient(0)
    gradient(1)

    for h in range(H):
        wait_bytes(out16.at[:, h], o_r.at[h])
    both = jnp.concatenate([out16[:, h].reshape(8 * 16, IH) for h in range(H)], axis=1)
    src = lax.broadcasted_iota(jnp.int32, (H * IH, H * IH), 0)
    dst = lax.broadcasted_iota(jnp.int32, (H * IH, H * IH), 1)
    place = (dst // ROWS) * RH + ((dst % ROWS) // RH) * IH + dst % RH
    order = jnp.where(src == place, 1.0, 0.0).astype(BF)
    ordered = jnp.dot(both, order, preferred_element_type=F32)
    for k in range(8):
        rows16 = ordered[k * 16 : (k + 1) * 16]
        pick = jnp.where(y == 0, rows16[0:4], 0.0)
        for y2 in range(1, NY):
            pick = jnp.where(y == y2, rows16[4 * y2 : 4 * y2 + 4], pick)
        resid_out[:, k * H * IH : (k + 1) * H * IH] = pick.astype(BF)

    wait_bytes(tok_recv, tok_s.at[0])
    wait_bytes(tokens.at[pl.ds(0, ND - 1), 0], tok_s.at[2])
    wait_bytes(tokens.at[:, 0], tok_s.at[4])
    wait_bytes(lsum, l_s)
    for k in range(NK):
        for m in range(2):
            wait_bytes(wrecv[k].at[m, pl.ds(0, 31)], w_s.at[m, k])
            wait_bytes(psum[k][m], p_s.at[m, k])
        wait_bytes(s.at[0, pl.ds(0, 3 * TQ), step_cols(k)], s_s.at[k])
        wait_bytes(s.at[0, :, step_cols(k)], f_s.at[k])
    for h in range(H):
        wait_bytes(wd.at[h, pl.ds(0, ND - 1)], d_s.at[h])
        wait_bytes(rr.at[h], rp_s.at[h])
        wait_bytes(rfull.at[h, pl.ds(0, ND - 1)], ra_s.at[h])
        wait_bytes(out16.at[pl.ds(0, 7), h], o_s.at[h])
        wait_bytes(gs.at[h, pl.ds(0, ND - 1)], g_s.at[h])
        wait_bytes(grad_out.at[pl.ds(h * RH, RH)], g_r.at[h])


def per_device(tokens, gate_weight, up_weight, down_weight_t, router, cluster_ids):
    dma = pltpu.SemaphoreType.DMA
    nk = NK
    hbm = pl.BlockSpec(memory_space=pltpu.HBM)
    vmem = pl.BlockSpec(memory_space=pltpu.VMEM)
    smem = pl.BlockSpec(memory_space=pltpu.SMEM)
    return pl.pallas_call(
        kernel,
        out_shape=(
            pltpu.VMEM((TOKENS // 128, D), BF),
            pltpu.VMEM((ROWS, FF), BF),
        ),
        in_specs=[hbm, hbm, hbm, hbm, hbm, smem],
        out_specs=(vmem, pl.BlockSpec(memory_space=pl.ANY)),
        scratch_shapes=[
            pltpu.VMEM((TOKENS // 128, D), BF),
            pltpu.VMEM((EXPERTS, KD), BF),
            pltpu.VMEM((NY, 16, KD), BF),
            pltpu.VMEM((NY - 1, 16, KD), BF),
            pltpu.VMEM((ND, 2, 16, KD), BF),
            tuple(pltpu.VMEM((2, 32, ROWS, n * BLOCK), BF) for n in CHUNKS),
            tuple(tuple(pltpu.VMEM((TOKENS, n * BLOCK), t) for t in ts) for n, ts in zip(CHUNKS, SENT)),
            tuple(tuple(pltpu.VMEM((TOKENS, n * BLOCK), F32) for _ in range(2)) for n in CHUNKS),
            tuple(tuple(pltpu.VMEM((NY - 1, TQ, n * BLOCK), t) for t in ts) for n, ts in zip(CHUNKS, SENT)),
            pltpu.VMEM((TOKENS, 128), F32),
            pltpu.VMEM((NY - 1, TQ, 128), F32),
            pltpu.VMEM((2, TOKENS, FC), BF),
            pltpu.VMEM((H, ND, RH, FD), BF),
            pltpu.VMEM((H, ND, 32, IH), BF),
            pltpu.VMEM((H, ND - 1, 32, IH), BF),
            pltpu.VMEM((H, ND, 32, IH), BF),
            pltpu.VMEM((8, H, 16, IH), BF),
            pltpu.VMEM((H, ND, RH, FD), BF),
            dma((2,)),
            dma((6,)),
            dma((2, nk)), dma((2, nk)),
            dma((2, nk)), dma((2, nk)),
            dma, dma,
            dma((nk,)), dma((nk,)),
            dma((nk,)), dma((nk,)),
            dma((H,)), dma((H,)),
            dma((H,)), dma((H,)),
            dma((H,)), dma((H,)),
            dma((H,)), dma((H,)),
            dma((H,)), dma((H,)),
        ],
        compiler_params=pltpu.CompilerParams(
            collective_id=0, has_side_effects=True, vmem_limit_bytes=54 * 2**20
        ),
    )(tokens, gate_weight, up_weight, down_weight_t, router.T, cluster_ids)


def solution(mesh):
    split = P(("expert", "dp"), None)
    return jax.shard_map(
        per_device,
        mesh=mesh,
        in_specs=(split, split, split, split, P(), P()),
        out_specs=(split, split),
        check_vma=False,
    )
```

```python
import jax
import jax.numpy as jnp
from jax import lax
from jax.experimental import pallas as pl
from jax.experimental.pallas import tpu as pltpu
from jax.sharding import PartitionSpec as P

MESH = pl.DeviceIdType.MESH
BF = jnp.bfloat16
F32 = jnp.float32

D = 4096
FF = 28672
EXPERTS = 16
BLOCK = 128
TOKENS = 512
NY = 4
ND = 16
ROWS = 32
KD = D // NY
FD = FF // ND
FC = FD // 2
CHUNKS = (2, 2, 2, 1)
STARTS = (0, 2, 4, 6)
NK = len(CHUNKS)
SENT = ((F32, BF), (F32, BF), (F32, BF), (F32, BF))
H = 2
RH = ROWS // H
IH = ND * RH
TQ = TOKENS // NY
PLAN = (
    ("I", 0, 2), ("I", 1, 2), ("P", 0, 0), ("P", 1, 0), ("I", 0, 3), ("I", 1, 3), ("D", 0), ("D", 1), ("L",),
    ("P", 0, 1), ("P", 1, 1), ("H", 0), ("P", 0, 2), ("P", 1, 2), ("H", 1), ("F", 0),
    ("P", 0, 3), ("P", 1, 3), ("H", 2), ("F", 1), ("H", 3), ("F", 2), ("F", 3),
)
DOWN_CUTS = (((0, 896), (896, 896)), ((0, 896), (896, 896)))
GRAD_CUTS = ((((0, 256), (256, 640)), ((0, 896),)), (((0, 896),), ((0, 512), (512, 384))))
OFFSETS = (
    (2, 2), (2, 1), (2, 3), (1, 2), (3, 2), (2, 0), (0, 2), (1, 1),
    (3, 3), (1, 3), (3, 1), (1, 0), (3, 0), (0, 1), (0, 3),
)
INV_ROOT = 1.0 / float(TOKENS) ** 0.5


def div(a, b):
    return lax.div(a, jnp.int32(b))


def rem(a, b):
    return lax.rem(a, jnp.int32(b))


def local_copy(src, dst, sem):
    return pltpu.make_async_copy(src, dst, sem)


def wait_bytes(ref, sem):
    pltpu.make_async_copy(ref, ref, sem).wait()


def kernel(
    tok_in, gw, uw, dw, router_in, ids,
    resid_out, grad_out,
    tok, router, tok_send, tok_recv, tokens, wrecv, part, own, psum, logit, lsum, s, wd, p, rr, rfull, out16, gs,
    in_s, tok_s, w_s, w_r, p_s, p_r, l_s, l_r, s_s, s_r, f_s, f_r, d_s, d_r, rp_s, rp_r, ra_s, ra_r, o_s, o_r, g_s, g_r,
):
    e = lax.axis_index("expert")
    d = lax.axis_index("dp")
    y, c = div(e, 2), rem(e, 2)
    x, z = div(d, 4), rem(d, 4)

    def plane_peer(o):
        if isinstance(o, tuple):
            return rem(x + o[0], 4) * 4 + rem(z + o[1], 4)
        return rem(x + div(o, 4), 4) * 4 + rem(z + rem(o, 4), 4)

    def each_peer(body):
        for offset in OFFSETS:
            body(offset)

    def remote(src, dst, ssem, rsem, te, td):
        pltpu.make_async_remote_copy(
            src, dst, ssem, rsem, device_id=(te, td), device_id_type=MESH
        ).start()

    def each(lo, hi, body):
        def step(o, carry):
            body(o)
            return carry

        lax.fori_loop(lo, hi, step, 0)

    bar = pltpu.get_barrier_semaphore()

    def greet_plane(o):
        pl.semaphore_signal(
            bar, inc=1, device_id=(y * 2 + rem(c + rem(o, 2), 2), plane_peer(div(o, 2))), device_id_type=MESH
        )

    each(1, 32, greet_plane)

    def greet_others(o):
        y2 = rem(y + 1 + div(o, 2), 4)
        pl.semaphore_signal(bar, inc=1, device_id=(y2 * 2 + rem(o, 2), d), device_id_type=MESH)

    each(0, 6, greet_others)

    tok_copy = local_copy(tok_in, tok, in_s.at[0])
    tok_copy.start()
    router_copy = local_copy(
        router_in.at[:, pl.ds(pl.multiple_of(y * KD, KD), KD)], router, in_s.at[1]
    )
    router_copy.start()

    pl.semaphore_wait(bar, 37)

    def issue_gu(m, k):
        w = (gw, uw)[m]
        n, first = CHUNKS[k], STARTS[k]
        me = c * ND + d

        def cols(c2, d2):
            return pl.ds(pl.multiple_of(d2 * FD + c2 * FC + first * BLOCK, BLOCK), n * BLOCK)

        def body(o):
            c2, d2 = rem(c + o[2], 2), plane_peer(o[:2])
            remote(w.at[:, cols(c2, d2)], wrecv[k].at[m, me], w_s.at[m, k], w_r.at[m, k], y * 2 + c2, d2)

        for other in range(2):
            for offset in OFFSETS:
                body(offset + (other,))
        body((0, 0, 1))
        local_copy(w.at[:, cols(c, d)], wrecv[k].at[m, me], w_r.at[m, k]).start()

    def issue_down(h):
        rows = pl.ds(h * RH, RH)
        for first, width in DOWN_CUTS[h]:

            def cols(d2):
                return pl.ds(pl.multiple_of(d2 * FD + first, BLOCK), width)

            to = wd.at[h, d, :, pl.ds(first, width)]

            def body(o):
                d2 = plane_peer(o)
                remote(dw.at[rows, cols(d2)], to, d_s.at[h], d_r.at[h], e, d2)

            each_peer(body)
            local_copy(dw.at[rows, cols(d)], to, d_r.at[h]).start()

    issue_gu(0, 0)

    tok_copy.wait()
    t = tok[...].astype(F32)
    t16 = jnp.concatenate([t] * 4, axis=0)
    row = lax.broadcasted_iota(jnp.int32, t16.shape, 0)
    t16 = jnp.where(row // 4 == y, t16, 0.0).astype(BF)
    for k in range(NY):
        tok_send[k] = t16[:, k * KD : (k + 1) * KD]

    def send_tok_col(o):
        y2 = rem(y + o, 4)
        remote(tok_send.at[y2], tok_recv.at[o - 1], tok_s.at[0], tok_s.at[1], y2 * 2 + c, d)

    each(1, NY, send_tok_col)

    wait_bytes(tok_recv, tok_s.at[1])
    mine = tok_send[y].astype(F32)
    for k in range(NY - 1):
        mine = mine + tok_recv[k].astype(F32)
    tokens[d, c] = mine.astype(BF)

    def send_tok_plane(o):
        remote(tokens.at[d, c], tokens.at[d, c], tok_s.at[2], tok_s.at[3], e, plane_peer(o))

    each_peer(send_tok_plane)
    issue_gu(1, 0)
    issue_gu(0, 1)
    wait_bytes(tokens.at[pl.ds(0, ND - 1), 0], tok_s.at[3])
    remote(tokens.at[:, c], tokens.at[:, c], tok_s.at[4], tok_s.at[5], y * 2 + 1 - c, d)
    issue_gu(1, 1)
    wait_bytes(tokens.at[:, 0], tok_s.at[5])
    rows_all = tokens[...].reshape(TOKENS, KD)

    router_copy.wait()
    logit[...] = jnp.zeros_like(logit)
    logit[:, :EXPERTS] = lax.dot_general(
        rows_all, router[...], (((1,), (1,)), ((), ())), preferred_element_type=F32
    )

    def rows_of(y2):
        return pl.ds(pl.multiple_of(y2 * TQ, TQ), TQ)

    def send_logit(o):
        y2 = rem(y + o, 4)
        remote(logit.at[rows_of(y2)], lsum.at[o - 1], l_s, l_r, y2 * 2 + c, d)

    each(1, NY, send_logit)

    def partial(m, k):
        n = CHUNKS[k]
        wait_bytes(wrecv[k].at[m], w_r.at[m, k])
        got = wrecv[k][m].reshape(KD, n * BLOCK)
        dot = jnp.dot(rows_all, got, preferred_element_type=F32)
        if SENT[k][m] == F32:
            part[k][m][...] = dot
        else:
            part[k][m][...] = dot.astype(BF)
            own[k][m][...] = dot

        def send(o):
            y2 = rem(y + o, 4)
            remote(part[k][m].at[rows_of(y2)], psum[k][m].at[o - 1], p_s.at[m, k], p_r.at[m, k], y2 * 2 + c, d)

        each(1, NY, send)

    def step_cols(k):
        return pl.ds(STARTS[k] * BLOCK, CHUNKS[k] * BLOCK)

    def hidden(k):
        n, first = CHUNKS[k], STARTS[k]
        sums = []
        for m in range(2):
            wait_bytes(psum[k][m], p_r.at[m, k])
            kept = part[k][m] if SENT[k][m] == F32 else own[k][m]
            total = kept[rows_of(y)]
            for o in range(NY - 1):
                total = total + psum[k][m][o].astype(F32)
            sums.append(total)
        lane = lax.broadcasted_iota(jnp.int32, (TQ, EXPERTS), 1)
        for j in range(n):
            expert = ids[d * (FD // BLOCK) + c * (FC // BLOCK) + first + j]
            scale = jnp.sum(jnp.where(lane == expert, gate_scale, 0.0), axis=1, keepdims=True)
            g = sums[0][:, j * BLOCK : (j + 1) * BLOCK]
            u = sums[1][:, j * BLOCK : (j + 1) * BLOCK]
            col = (first + j) * BLOCK
            s[c, rows_of(y), col : col + BLOCK] = (scale * (g * jax.nn.sigmoid(g) * u)).astype(BF)
        view = s.at[c, rows_of(y), step_cols(k)]

        def send(o):
            remote(view, view, s_s.at[k], s_r.at[k], rem(y + o, 4) * 2 + c, d)

        each(1, NY, send)

    def hand_over(k):
        wait_bytes(s.at[0, pl.ds(0, 3 * TQ), step_cols(k)], s_r.at[k])
        view = s.at[c, :, step_cols(k)]
        remote(view, view, f_s.at[k], f_r.at[k], y * 2 + 1 - c, d)

    for op in PLAN:
        if op[0] == "I":
            issue_gu(*op[1:])
        elif op[0] == "D":
            issue_down(op[1])
        elif op[0] == "P":
            partial(*op[1:])
        elif op[0] == "L":
            wait_bytes(lsum, l_r)
            total = logit[rows_of(y), :EXPERTS]
            for o in range(NY - 1):
                total = total + lsum[o][:, :EXPERTS]
            gate_scale = 2.0 * jax.nn.sigmoid(total) - 1.0
        elif op[0] == "H":
            hidden(op[1])
        else:
            hand_over(op[1])
    for k in range(NK):
        wait_bytes(s.at[0, :, step_cols(k)], f_r.at[k])

    def residual(h):
        wait_bytes(wd.at[h], d_r.at[h])
        w = wd[h].reshape(IH, FD)
        acc = lax.dot_general(s[0], w[:, :FC], (((1,), (1,)), ((), ())), preferred_element_type=F32)
        acc = acc + lax.dot_general(s[1], w[:, FC:], (((1,), (1,)), ((), ())), preferred_element_type=F32)
        p[h] = acc.astype(BF).reshape(ND, 32, IH)

        def send(o):
            d2 = plane_peer(o)
            remote(p.at[h, d2], rr.at[h, OFFSETS.index(o)], rp_s.at[h], rp_r.at[h], e, d2)

        each_peer(send)

    def reduce_residual(h):
        wait_bytes(rr.at[h], rp_r.at[h])
        acc = p[h, d].astype(F32)
        for o in range(ND - 1):
            acc = acc + rr[h, o].astype(F32)
        rfull[h, d] = acc.astype(BF)
        view = rfull.at[h, d]

        def send(o):
            remote(view, view, ra_s.at[h], ra_r.at[h], e, plane_peer(o))

        each_peer(send)

    def send_rows(h):
        def send_out(o):
            e2 = rem(e + o, 8)
            rows = pl.ds(pl.multiple_of(rem(e2, 2) * 16, 16), 16)
            remote(rfull.at[h, d, rows], out16.at[e, h], o_s.at[h], o_r.at[h], e2, d)

        each(1, 8, send_out)
        rows = pl.ds(pl.multiple_of(c * 16, 16), 16)
        local_copy(rfull.at[h, d, rows], out16.at[e, h], o_r.at[h]).start()

    def gradient(h):
        wait_bytes(rfull.at[h, pl.ds(0, ND - 1)], ra_r.at[h])
        r = rfull[h].reshape(TOKENS, IH)
        rows = pl.ds(h * RH, RH)
        for c2 in range(2):
            for first, width in GRAD_CUTS[h][c2]:
                dot = lax.dot_general(
                    r, s[c2, :, first : first + width], (((0,), (0,)), ((), ())), preferred_element_type=F32
                )
                cols = pl.ds(pl.multiple_of(d * FD + c2 * FC + first, BLOCK), width)
                part_cols = pl.ds(c2 * FC + first, width)
                gs[h, :, :, part_cols] = (dot * INV_ROOT).astype(BF).reshape(ND, RH, width)

                def send(o):
                    d2 = plane_peer(o)
                    remote(gs.at[h, d2, :, part_cols], grad_out.at[rows, cols], g_s.at[h], g_r.at[h], e, d2)

                each_peer(send)
                local_copy(gs.at[h, d, :, part_cols], grad_out.at[rows, cols], g_r.at[h]).start()

    residual(0)
    residual(1)
    reduce_residual(0)
    reduce_residual(1)
    gradient(0)
    gradient(1)
    send_rows(0)
    send_rows(1)

    for h in range(H):
        wait_bytes(out16.at[:, h], o_r.at[h])
    both = jnp.concatenate([out16[:, h].reshape(8 * 16, IH) for h in range(H)], axis=1)
    src = lax.broadcasted_iota(jnp.int32, (H * IH, H * IH), 0)
    dst = lax.broadcasted_iota(jnp.int32, (H * IH, H * IH), 1)
    place = (dst // ROWS) * RH + ((dst % ROWS) // RH) * IH + dst % RH
    order = jnp.where(src == place, 1.0, 0.0).astype(BF)
    ordered = jnp.dot(both, order, preferred_element_type=F32)
    for k in range(8):
        rows16 = ordered[k * 16 : (k + 1) * 16]
        pick = jnp.where(y == 0, rows16[0:4], 0.0)
        for y2 in range(1, NY):
            pick = jnp.where(y == y2, rows16[4 * y2 : 4 * y2 + 4], pick)
        resid_out[:, k * H * IH : (k + 1) * H * IH] = pick.astype(BF)

    wait_bytes(tok_recv, tok_s.at[0])
    wait_bytes(tokens.at[pl.ds(0, ND - 1), 0], tok_s.at[2])
    wait_bytes(tokens.at[:, 0], tok_s.at[4])
    wait_bytes(lsum, l_s)
    for k in range(NK):
        for m in range(2):
            wait_bytes(wrecv[k].at[m, pl.ds(0, 31)], w_s.at[m, k])
            wait_bytes(psum[k][m], p_s.at[m, k])
        wait_bytes(s.at[0, pl.ds(0, 3 * TQ), step_cols(k)], s_s.at[k])
        wait_bytes(s.at[0, :, step_cols(k)], f_s.at[k])
    for h in range(H):
        wait_bytes(wd.at[h, pl.ds(0, ND - 1)], d_s.at[h])
        wait_bytes(rr.at[h], rp_s.at[h])
        wait_bytes(rfull.at[h, pl.ds(0, ND - 1)], ra_s.at[h])
        wait_bytes(out16.at[pl.ds(0, 7), h], o_s.at[h])
        wait_bytes(gs.at[h, pl.ds(0, ND - 1)], g_s.at[h])
        wait_bytes(grad_out.at[pl.ds(h * RH, RH)], g_r.at[h])


def per_device(tokens, gate_weight, up_weight, down_weight_t, router, cluster_ids):
    dma = pltpu.SemaphoreType.DMA
    nk = NK
    hbm = pl.BlockSpec(memory_space=pltpu.HBM)
    vmem = pl.BlockSpec(memory_space=pltpu.VMEM)
    smem = pl.BlockSpec(memory_space=pltpu.SMEM)
    return pl.pallas_call(
        kernel,
        out_shape=(
            pltpu.VMEM((TOKENS // 128, D), BF),
            pltpu.VMEM((ROWS, FF), BF),
        ),
        in_specs=[hbm, hbm, hbm, hbm, hbm, smem],
        out_specs=(vmem, pl.BlockSpec(memory_space=pl.ANY)),
        scratch_shapes=[
            pltpu.VMEM((TOKENS // 128, D), BF),
            pltpu.VMEM((EXPERTS, KD), BF),
            pltpu.VMEM((NY, 16, KD), BF),
            pltpu.VMEM((NY - 1, 16, KD), BF),
            pltpu.VMEM((ND, 2, 16, KD), BF),
            tuple(pltpu.VMEM((2, 32, ROWS, n * BLOCK), BF) for n in CHUNKS),
            tuple(tuple(pltpu.VMEM((TOKENS, n * BLOCK), t) for t in ts) for n, ts in zip(CHUNKS, SENT)),
            tuple(tuple(pltpu.VMEM((TOKENS, n * BLOCK), F32) for _ in range(2)) for n in CHUNKS),
            tuple(tuple(pltpu.VMEM((NY - 1, TQ, n * BLOCK), t) for t in ts) for n, ts in zip(CHUNKS, SENT)),
            pltpu.VMEM((TOKENS, 128), F32),
            pltpu.VMEM((NY - 1, TQ, 128), F32),
            pltpu.VMEM((2, TOKENS, FC), BF),
            pltpu.VMEM((H, ND, RH, FD), BF),
            pltpu.VMEM((H, ND, 32, IH), BF),
            pltpu.VMEM((H, ND - 1, 32, IH), BF),
            pltpu.VMEM((H, ND, 32, IH), BF),
            pltpu.VMEM((8, H, 16, IH), BF),
            pltpu.VMEM((H, ND, RH, FD), BF),
            dma((2,)),
            dma((6,)),
            dma((2, nk)), dma((2, nk)),
            dma((2, nk)), dma((2, nk)),
            dma, dma,
            dma((nk,)), dma((nk,)),
            dma((nk,)), dma((nk,)),
            dma((H,)), dma((H,)),
            dma((H,)), dma((H,)),
            dma((H,)), dma((H,)),
            dma((H,)), dma((H,)),
            dma((H,)), dma((H,)),
        ],
        compiler_params=pltpu.CompilerParams(
            collective_id=0, has_side_effects=True, vmem_limit_bytes=54 * 2**20
        ),
    )(tokens, gate_weight, up_weight, down_weight_t, router.T, cluster_ids)


def solution(mesh):
    split = P(("expert", "dp"), None)
    return jax.shard_map(
        per_device,
        mesh=mesh,
        in_specs=(split, split, split, split, P(), P()),
        out_specs=(split, split),
        check_vma=False,
    )
```

```python
import jax
import jax.numpy as jnp
from jax import lax
from jax.experimental import pallas as pl
from jax.experimental.pallas import tpu as pltpu
from jax.sharding import PartitionSpec as P

MESH = pl.DeviceIdType.MESH
BF = jnp.bfloat16
F32 = jnp.float32

D = 4096
FF = 28672
EXPERTS = 16
BLOCK = 128
TOKENS = 512
NY = 4
ND = 16
ROWS = 32
KD = D // NY
FD = FF // ND
FC = FD // 2
CHUNKS = (2, 2, 2, 1)
STARTS = (0, 2, 4, 6)
NK = len(CHUNKS)
SENT = ((F32, BF), (F32, BF), (F32, BF), (F32, BF))
H = 2
RH = ROWS // H
IH = ND * RH
TQ = TOKENS // NY
PLAN = (
    ("I", 0, 2), ("I", 1, 2), ("P", 0, 0), ("P", 1, 0), ("I", 0, 3), ("I", 1, 3), ("D", 0), ("D", 1), ("L",),
    ("P", 0, 1), ("P", 1, 1), ("H", 0), ("P", 0, 2), ("P", 1, 2), ("H", 1), ("F", 0),
    ("P", 0, 3), ("P", 1, 3), ("H", 2), ("F", 1), ("H", 3), ("F", 2), ("F", 3),
)
DOWN_CUTS = (((0, 896), (896, 896)), ((0, 896), (896, 896)))
GRAD_CUTS = ((((0, 256), (256, 640)), ((0, 896),)), (((0, 896),), ((0, 512), (512, 384))))
OFFSETS = (
    (2, 2), (2, 1), (2, 3), (1, 2), (3, 2), (2, 0), (0, 2), (1, 1),
    (3, 3), (1, 3), (3, 1), (1, 0), (3, 0), (0, 1), (0, 3),
)
INV_ROOT = 1.0 / float(TOKENS) ** 0.5


def div(a, b):
    return lax.div(a, jnp.int32(b))


def rem(a, b):
    return lax.rem(a, jnp.int32(b))


def local_copy(src, dst, sem):
    return pltpu.make_async_copy(src, dst, sem)


def wait_bytes(ref, sem):
    pltpu.make_async_copy(ref, ref, sem).wait()


def kernel(
    tok_in, gw, uw, dw, router_in, ids,
    resid_out, grad_out,
    tok, router, tok_send, tok_recv, tokens, wrecv, part, own, psum, logit, lsum, s, wd, p, rr, rfull, out16, gs,
    in_s, tok_s, w_s, w_r, p_s, p_r, l_s, l_r, s_s, s_r, f_s, f_r, d_s, d_r, rp_s, rp_r, ra_s, ra_r, o_s, o_r, g_s, g_r,
):
    e = lax.axis_index("expert")
    d = lax.axis_index("dp")
    y, c = div(e, 2), rem(e, 2)
    x, z = div(d, 4), rem(d, 4)

    def plane_peer(o):
        if isinstance(o, tuple):
            return rem(x + o[0], 4) * 4 + rem(z + o[1], 4)
        return rem(x + div(o, 4), 4) * 4 + rem(z + rem(o, 4), 4)

    def each_peer(body):
        for offset in OFFSETS:
            body(offset)

    def remote(src, dst, ssem, rsem, te, td):
        pltpu.make_async_remote_copy(
            src, dst, ssem, rsem, device_id=(te, td), device_id_type=MESH
        ).start()

    def each(lo, hi, body):
        def step(o, carry):
            body(o)
            return carry

        lax.fori_loop(lo, hi, step, 0)

    bar = pltpu.get_barrier_semaphore()

    def greet_plane(o):
        pl.semaphore_signal(
            bar, inc=1, device_id=(y * 2 + rem(c + rem(o, 2), 2), plane_peer(div(o, 2))), device_id_type=MESH
        )

    each(1, 32, greet_plane)

    def greet_others(o):
        y2 = rem(y + 1 + div(o, 2), 4)
        pl.semaphore_signal(bar, inc=1, device_id=(y2 * 2 + rem(o, 2), d), device_id_type=MESH)

    each(0, 6, greet_others)

    tok_copy = local_copy(tok_in, tok, in_s.at[0])
    tok_copy.start()
    router_copy = local_copy(
        router_in.at[:, pl.ds(pl.multiple_of(y * KD, KD), KD)], router, in_s.at[1]
    )
    router_copy.start()

    tok_copy.wait()
    t = tok[...].astype(F32)
    t16 = jnp.concatenate([t] * 4, axis=0)
    row = lax.broadcasted_iota(jnp.int32, t16.shape, 0)
    t16 = jnp.where(row // 4 == y, t16, 0.0).astype(BF)
    for k in range(NY):
        tok_send[k] = t16[:, k * KD : (k + 1) * KD]

    pl.semaphore_wait(bar, 37)

    def send_tok_col(o):
        y2 = rem(y + o, 4)
        remote(tok_send.at[y2], tok_recv.at[o - 1], tok_s.at[0], tok_s.at[1], y2 * 2 + c, d)

    each(1, NY, send_tok_col)


    def issue_gu(m, k):
        w = (gw, uw)[m]
        n, first = CHUNKS[k], STARTS[k]
        me = c * ND + d

        def cols(c2, d2):
            return pl.ds(pl.multiple_of(d2 * FD + c2 * FC + first * BLOCK, BLOCK), n * BLOCK)

        def body(o):
            c2, d2 = rem(c + o[2], 2), plane_peer(o[:2])
            remote(w.at[:, cols(c2, d2)], wrecv[k].at[m, me], w_s.at[m, k], w_r.at[m, k], y * 2 + c2, d2)

        for other in range(2):
            for offset in OFFSETS:
                body(offset + (other,))
        body((0, 0, 1))
        local_copy(w.at[:, cols(c, d)], wrecv[k].at[m, me], w_r.at[m, k]).start()

    def issue_down(h):
        rows = pl.ds(h * RH, RH)
        for first, width in DOWN_CUTS[h]:

            def cols(d2):
                return pl.ds(pl.multiple_of(d2 * FD + first, BLOCK), width)

            to = wd.at[h, d, :, pl.ds(first, width)]

            def body(o):
                d2 = plane_peer(o)
                remote(dw.at[rows, cols(d2)], to, d_s.at[h], d_r.at[h], e, d2)

            each_peer(body)
            local_copy(dw.at[rows, cols(d)], to, d_r.at[h]).start()

    issue_gu(0, 0)

    wait_bytes(tok_recv, tok_s.at[1])
    mine = tok_send[y].astype(F32)
    for k in range(NY - 1):
        mine = mine + tok_recv[k].astype(F32)
    tokens[d, c] = mine.astype(BF)

    def send_tok_plane(o):
        remote(tokens.at[d, c], tokens.at[d, c], tok_s.at[2], tok_s.at[3], e, plane_peer(o))

    each_peer(send_tok_plane)
    issue_gu(1, 0)
    issue_gu(0, 1)
    wait_bytes(tokens.at[pl.ds(0, ND - 1), 0], tok_s.at[3])
    remote(tokens.at[:, c], tokens.at[:, c], tok_s.at[4], tok_s.at[5], y * 2 + 1 - c, d)
    issue_gu(1, 1)
    wait_bytes(tokens.at[:, 0], tok_s.at[5])
    rows_all = tokens[...].reshape(TOKENS, KD)

    router_copy.wait()
    logit[...] = jnp.zeros_like(logit)
    logit[:, :EXPERTS] = lax.dot_general(
        rows_all, router[...], (((1,), (1,)), ((), ())), preferred_element_type=F32
    )

    def rows_of(y2):
        return pl.ds(pl.multiple_of(y2 * TQ, TQ), TQ)

    def send_logit(o):
        y2 = rem(y + o, 4)
        remote(logit.at[rows_of(y2)], lsum.at[o - 1], l_s, l_r, y2 * 2 + c, d)

    each(1, NY, send_logit)

    def partial(m, k):
        n = CHUNKS[k]
        wait_bytes(wrecv[k].at[m], w_r.at[m, k])
        got = wrecv[k][m].reshape(KD, n * BLOCK)
        dot = jnp.dot(rows_all, got, preferred_element_type=F32)
        if SENT[k][m] == F32:
            part[k][m][...] = dot
        else:
            part[k][m][...] = dot.astype(BF)
            own[k][m][...] = dot

        def send(o):
            y2 = rem(y + o, 4)
            remote(part[k][m].at[rows_of(y2)], psum[k][m].at[o - 1], p_s.at[m, k], p_r.at[m, k], y2 * 2 + c, d)

        each(1, NY, send)

    def step_cols(k):
        return pl.ds(STARTS[k] * BLOCK, CHUNKS[k] * BLOCK)

    def hidden(k):
        n, first = CHUNKS[k], STARTS[k]
        sums = []
        for m in range(2):
            wait_bytes(psum[k][m], p_r.at[m, k])
            kept = part[k][m] if SENT[k][m] == F32 else own[k][m]
            total = kept[rows_of(y)]
            for o in range(NY - 1):
                total = total + psum[k][m][o].astype(F32)
            sums.append(total)
        lane = lax.broadcasted_iota(jnp.int32, (TQ, EXPERTS), 1)
        for j in range(n):
            expert = ids[d * (FD // BLOCK) + c * (FC // BLOCK) + first + j]
            scale = jnp.sum(jnp.where(lane == expert, gate_scale, 0.0), axis=1, keepdims=True)
            g = sums[0][:, j * BLOCK : (j + 1) * BLOCK]
            u = sums[1][:, j * BLOCK : (j + 1) * BLOCK]
            col = (first + j) * BLOCK
            s[c, rows_of(y), col : col + BLOCK] = (scale * (g * jax.nn.sigmoid(g) * u)).astype(BF)
        view = s.at[c, rows_of(y), step_cols(k)]

        def send(o):
            remote(view, view, s_s.at[k], s_r.at[k], rem(y + o, 4) * 2 + c, d)

        each(1, NY, send)

    def hand_over(k):
        wait_bytes(s.at[0, pl.ds(0, 3 * TQ), step_cols(k)], s_r.at[k])
        view = s.at[c, :, step_cols(k)]
        remote(view, view, f_s.at[k], f_r.at[k], y * 2 + 1 - c, d)

    for op in PLAN:
        if op[0] == "I":
            issue_gu(*op[1:])
        elif op[0] == "D":
            issue_down(op[1])
        elif op[0] == "P":
            partial(*op[1:])
        elif op[0] == "L":
            wait_bytes(lsum, l_r)
            total = logit[rows_of(y), :EXPERTS]
            for o in range(NY - 1):
                total = total + lsum[o][:, :EXPERTS]
            gate_scale = 2.0 * jax.nn.sigmoid(total) - 1.0
        elif op[0] == "H":
            hidden(op[1])
        else:
            hand_over(op[1])
    for k in range(NK):
        wait_bytes(s.at[0, :, step_cols(k)], f_r.at[k])

    def residual(h):
        wait_bytes(wd.at[h], d_r.at[h])
        w = wd[h].reshape(IH, FD)
        acc = lax.dot_general(s[0], w[:, :FC], (((1,), (1,)), ((), ())), preferred_element_type=F32)
        acc = acc + lax.dot_general(s[1], w[:, FC:], (((1,), (1,)), ((), ())), preferred_element_type=F32)
        p[h] = acc.astype(BF).reshape(ND, 32, IH)

        def send(o):
            d2 = plane_peer(o)
            remote(p.at[h, d2], rr.at[h, OFFSETS.index(o)], rp_s.at[h], rp_r.at[h], e, d2)

        each_peer(send)

    def reduce_residual(h):
        wait_bytes(rr.at[h], rp_r.at[h])
        acc = p[h, d].astype(F32)
        for o in range(ND - 1):
            acc = acc + rr[h, o].astype(F32)
        rfull[h, d] = acc.astype(BF)
        view = rfull.at[h, d]

        def send(o):
            remote(view, view, ra_s.at[h], ra_r.at[h], e, plane_peer(o))

        each_peer(send)

    def send_rows(h):
        def send_out(o):
            e2 = rem(e + o, 8)
            rows = pl.ds(pl.multiple_of(rem(e2, 2) * 16, 16), 16)
            remote(rfull.at[h, d, rows], out16.at[e, h], o_s.at[h], o_r.at[h], e2, d)

        each(1, 8, send_out)
        rows = pl.ds(pl.multiple_of(c * 16, 16), 16)
        local_copy(rfull.at[h, d, rows], out16.at[e, h], o_r.at[h]).start()

    def gradient(h):
        wait_bytes(rfull.at[h, pl.ds(0, ND - 1)], ra_r.at[h])
        r = rfull[h].reshape(TOKENS, IH)
        rows = pl.ds(h * RH, RH)
        for c2 in range(2):
            for first, width in GRAD_CUTS[h][c2]:
                dot = lax.dot_general(
                    r, s[c2, :, first : first + width], (((0,), (0,)), ((), ())), preferred_element_type=F32
                )
                cols = pl.ds(pl.multiple_of(d * FD + c2 * FC + first, BLOCK), width)
                part_cols = pl.ds(c2 * FC + first, width)
                gs[h, :, :, part_cols] = (dot * INV_ROOT).astype(BF).reshape(ND, RH, width)

                def send(o):
                    d2 = plane_peer(o)
                    remote(gs.at[h, d2, :, part_cols], grad_out.at[rows, cols], g_s.at[h], g_r.at[h], e, d2)

                each_peer(send)
                local_copy(gs.at[h, d, :, part_cols], grad_out.at[rows, cols], g_r.at[h]).start()

    residual(0)
    residual(1)
    reduce_residual(0)
    reduce_residual(1)
    gradient(0)
    gradient(1)
    send_rows(0)
    send_rows(1)

    for h in range(H):
        wait_bytes(out16.at[:, h], o_r.at[h])
    both = jnp.concatenate([out16[:, h].reshape(8 * 16, IH) for h in range(H)], axis=1)
    src = lax.broadcasted_iota(jnp.int32, (H * IH, H * IH), 0)
    dst = lax.broadcasted_iota(jnp.int32, (H * IH, H * IH), 1)
    place = (dst // ROWS) * RH + ((dst % ROWS) // RH) * IH + dst % RH
    order = jnp.where(src == place, 1.0, 0.0).astype(BF)
    ordered = jnp.dot(both, order, preferred_element_type=F32)
    for k in range(8):
        rows16 = ordered[k * 16 : (k + 1) * 16]
        pick = jnp.where(y == 0, rows16[0:4], 0.0)
        for y2 in range(1, NY):
            pick = jnp.where(y == y2, rows16[4 * y2 : 4 * y2 + 4], pick)
        resid_out[:, k * H * IH : (k + 1) * H * IH] = pick.astype(BF)

    wait_bytes(tok_recv, tok_s.at[0])
    wait_bytes(tokens.at[pl.ds(0, ND - 1), 0], tok_s.at[2])
    wait_bytes(tokens.at[:, 0], tok_s.at[4])
    wait_bytes(lsum, l_s)
    for k in range(NK):
        for m in range(2):
            wait_bytes(wrecv[k].at[m, pl.ds(0, 31)], w_s.at[m, k])
            wait_bytes(psum[k][m], p_s.at[m, k])
        wait_bytes(s.at[0, pl.ds(0, 3 * TQ), step_cols(k)], s_s.at[k])
        wait_bytes(s.at[0, :, step_cols(k)], f_s.at[k])
    for h in range(H):
        wait_bytes(wd.at[h, pl.ds(0, ND - 1)], d_s.at[h])
        wait_bytes(rr.at[h], rp_s.at[h])
        wait_bytes(rfull.at[h, pl.ds(0, ND - 1)], ra_s.at[h])
        wait_bytes(out16.at[pl.ds(0, 7), h], o_s.at[h])
        wait_bytes(gs.at[h, pl.ds(0, ND - 1)], g_s.at[h])
        wait_bytes(grad_out.at[pl.ds(h * RH, RH)], g_r.at[h])


def per_device(tokens, gate_weight, up_weight, down_weight_t, router, cluster_ids):
    dma = pltpu.SemaphoreType.DMA
    nk = NK
    hbm = pl.BlockSpec(memory_space=pltpu.HBM)
    vmem = pl.BlockSpec(memory_space=pltpu.VMEM)
    smem = pl.BlockSpec(memory_space=pltpu.SMEM)
    return pl.pallas_call(
        kernel,
        out_shape=(
            pltpu.VMEM((TOKENS // 128, D), BF),
            pltpu.VMEM((ROWS, FF), BF),
        ),
        in_specs=[hbm, hbm, hbm, hbm, hbm, smem],
        out_specs=(vmem, pl.BlockSpec(memory_space=pl.ANY)),
        scratch_shapes=[
            pltpu.VMEM((TOKENS // 128, D), BF),
            pltpu.VMEM((EXPERTS, KD), BF),
            pltpu.VMEM((NY, 16, KD), BF),
            pltpu.VMEM((NY - 1, 16, KD), BF),
            pltpu.VMEM((ND, 2, 16, KD), BF),
            tuple(pltpu.VMEM((2, 32, ROWS, n * BLOCK), BF) for n in CHUNKS),
            tuple(tuple(pltpu.VMEM((TOKENS, n * BLOCK), t) for t in ts) for n, ts in zip(CHUNKS, SENT)),
            tuple(tuple(pltpu.VMEM((TOKENS, n * BLOCK), F32) for _ in range(2)) for n in CHUNKS),
            tuple(tuple(pltpu.VMEM((NY - 1, TQ, n * BLOCK), t) for t in ts) for n, ts in zip(CHUNKS, SENT)),
            pltpu.VMEM((TOKENS, 128), F32),
            pltpu.VMEM((NY - 1, TQ, 128), F32),
            pltpu.VMEM((2, TOKENS, FC), BF),
            pltpu.VMEM((H, ND, RH, FD), BF),
            pltpu.VMEM((H, ND, 32, IH), BF),
            pltpu.VMEM((H, ND - 1, 32, IH), BF),
            pltpu.VMEM((H, ND, 32, IH), BF),
            pltpu.VMEM((8, H, 16, IH), BF),
            pltpu.VMEM((H, ND, RH, FD), BF),
            dma((2,)),
            dma((6,)),
            dma((2, nk)), dma((2, nk)),
            dma((2, nk)), dma((2, nk)),
            dma, dma,
            dma((nk,)), dma((nk,)),
            dma((nk,)), dma((nk,)),
            dma((H,)), dma((H,)),
            dma((H,)), dma((H,)),
            dma((H,)), dma((H,)),
            dma((H,)), dma((H,)),
            dma((H,)), dma((H,)),
        ],
        compiler_params=pltpu.CompilerParams(
            collective_id=0, has_side_effects=True, vmem_limit_bytes=54 * 2**20
        ),
    )(tokens, gate_weight, up_weight, down_weight_t, router.T, cluster_ids)


def solution(mesh):
    split = P(("expert", "dp"), None)
    return jax.shard_map(
        per_device,
        mesh=mesh,
        in_specs=(split, split, split, split, P(), P()),
        out_specs=(split, split),
        check_vma=False,
    )
```
